256 devices in a mesh: row: 8 (over x_lo, y), col: 32 (over x_hi, z, core).
Axes of the slice: x: 4 (x_hi: 2, x_lo: 2; x = x_hi * 2 + x_lo), y: 4, z: 8, core: 2. Of those that a mesh axis runs over, the one named last changes fastest.
Arguments:
- tokens: bfloat16 [512, 12288], P('col', 'row'), may hold values from -6 to 6
- w_up: bfloat16 [12288, 24576], P('row', 'col'), may hold values from -0.0546875 to 0.0546875
- w_down: bfloat16 [24576, 12288], P('col', 'row'), may hold values from -0.0390625 to 0.0390625
- grad_out: bfloat16 [512, 12288], P('col', 'row'), may hold values from -6 to 6
Outputs:
- output: bfloat16 [512, 12288], P('col', 'row')
- grad_tokens: bfloat16 [512, 12288], P('col', 'row')
- grad_up: bfloat16 [12288, 24576], P('row', 'col')
- grad_down: bfloat16 [24576, 12288], P('col', 'row')
The draws below stay inside these ranges and needn't reach their ends.
All inputs are finite; a program needn't handle non-finite values.
Results may differ from the reference program's by a relative error of at most 0.005.
Values may be sent and summed in bfloat16 or wider, within the bound.
No kernel may reach another device: no remote copies, remote signals or barrier semaphores. Data moves between devices by JAX's collectives and lax.ppermute only.
A program may use at most 64 MiB of HBM per device.

```python
import jax
import jax.numpy as jnp
from jax import lax

D = 12288
FF = 24576
TOKENS = 512


def steps_of(own_key, shape, split, least, high):
    gain = 1.0
    for position, parts in split:
        heights = jax.random.uniform(jax.random.fold_in(jax.random.fold_in(own_key, 6), position), (parts,), jnp.float32, least / len(split), high / len(split))
        gain = gain * jnp.repeat(jnp.exp(heights), shape[position] // parts).reshape((-1,) + (1,) * (len(shape) - 1 - position))
    return gain


def centred(own_key, dims, spread, limit, shards=(), held_as=jnp.bfloat16):
    factor_of = steps_of(own_key, dims, shards, -0.22, 0.18) if shards else 1.0
    result = jax.random.normal(own_key, dims, jnp.float32) * spread * factor_of
    return jnp.minimum(jnp.maximum(result, -limit), limit).astype(held_as)


def setup_inputs(seed: int = 0) -> dict:
    key_of = jax.random.split(jax.random.key(seed), 5)
    tokens = centred(key_of[0], (TOKENS, D), 1.0, 6.0, ((0, 32), (1, 8)))
    w_up = centred(key_of[1], (D, FF), D ** -0.5, 0.0546875, ((0, 8), (1, 32)))
    w_down = centred(key_of[2], (FF, D), FF ** -0.5, 0.0390625, ((0, 32), (1, 8)))
    grad_out = centred(key_of[3], (TOKENS, D), 1.0, 6.0, ((0, 32), (1, 8)))
    return {"tokens": tokens, "w_up": w_up, "w_down": w_down, "grad_out": grad_out}


gelu_coef = 0.7978845608028654


def gelu_pair(preact):
    tanh_val = jnp.tanh(gelu_coef * (preact + 0.044715 * preact * preact * preact))
    activated = 0.5 * preact * (1.0 + tanh_val)
    derivative = 0.5 * (1.0 + tanh_val) + 0.5 * preact * (1.0 - tanh_val * tanh_val) * gelu_coef * (1.0 + 3.0 * 0.044715 * preact * preact)
    return activated, derivative


def reference(tokens, w_up, w_down, grad_out):
    contract_last = (((1,), (1,)), ((), ()))
    contract_first = (((0,), (0,)), ((), ()))
    preact = jnp.dot(tokens, w_up, preferred_element_type=jnp.float32)
    back_grad = lax.dot_general(grad_out, w_down, contract_last, preferred_element_type=jnp.float32)
    activated, derivative = gelu_pair(preact)
    hidden = activated.astype(jnp.bfloat16)
    grad_pre = (back_grad * derivative).astype(jnp.bfloat16)
    output = jnp.dot(hidden, w_down, preferred_element_type=jnp.float32).astype(jnp.bfloat16)
    grad_tokens = lax.dot_general(grad_pre, w_up, contract_last, preferred_element_type=jnp.float32).astype(jnp.bfloat16)
    grad_scale = 1.0 / (TOKENS ** 0.5)
    grad_up = (lax.dot_general(tokens, grad_pre, contract_first, preferred_element_type=jnp.float32) * grad_scale).astype(jnp.bfloat16)
    grad_down = (lax.dot_general(hidden, grad_out, contract_first, preferred_element_type=jnp.float32) * grad_scale).astype(jnp.bfloat16)
    return (output, grad_tokens, grad_up, grad_down)
```

```python
import math

import jax
import jax.numpy as jnp
from jax import lax
from jax.sharding import PartitionSpec as P

gelu_coef = 0.7978845608028654


def activate(preact, back_grad):
    tanh_val = jnp.tanh(gelu_coef * (preact + 0.044715 * preact * preact * preact))
    activated = 0.5 * preact * (1.0 + tanh_val)
    derivative = 0.5 * (1.0 + tanh_val) + 0.5 * preact * (1.0 - tanh_val * tanh_val) * gelu_coef * (
        1.0 + 3.0 * 0.044715 * preact * preact
    )
    return (activated.astype(jnp.bfloat16), (back_grad * derivative).astype(jnp.bfloat16))


def perms(cols):
    ring = cols // 4

    def index(x_hi, z, core):
        return (x_hi * ring + z % ring) * 2 + core

    places = [(h, z, c) for h in range(2) for z in range(ring) for c in range(2)]
    swap_core = [(index(h, z, c), index(h, z, 1 - c)) for h, z, c in places]
    swap_half = [(index(h, z, c), index(1 - h, z, c)) for h, z, c in places]

    def pairing(phase):
        def partner(z, c):
            return z + 1 if (z + c + phase) % 2 == 0 else z - 1

        return [(index(h, z, c), index(h, partner(z, c), c)) for h, z, c in places]

    return swap_core, swap_half, pairing(0), pairing(1)


def local(swap_core, swap_half, even, odd, rows, tokens, w_up, w_down, grad_out):
    contract_last = (((1,), (1,)), ((), ()))
    contract_first = (((0,), (0,)), ((), ()))

    def swap(value, perm):
        return lax.ppermute(value, "col", perm)

    share = tokens.shape[0]
    feats = tokens.shape[1]
    total_rows = share * len(swap_core)
    hid = w_up.shape[1]
    grad_scale = 1.0 / math.sqrt(total_rows)

    mine = jnp.concatenate([tokens, grad_out], axis=1)
    unit = jnp.concatenate([mine, swap(mine, swap_half)], axis=0)
    first = jnp.concatenate([unit, swap(unit, even)], axis=0)
    second = swap(first, odd)
    third = swap(second, even)
    fourth = swap(third, odd)
    w_up_all = jnp.concatenate([w_up, swap(w_up, swap_core)], axis=1)
    w_down_all = jnp.concatenate([w_down, swap(w_down, swap_core)], axis=0)
    both = jnp.concatenate([first, second, third, fourth], axis=0)
    x_own, dy_own = both[:, :feats], both[:, feats:]
    units = both.shape[0] // rows

    preact = jnp.dot(x_own, w_up_all, preferred_element_type=jnp.float32).astype(jnp.bfloat16)
    back_grad = lax.dot_general(
        dy_own, w_down_all, contract_last, preferred_element_type=jnp.float32
    ).astype(jnp.bfloat16)
    parts = jnp.stack(
        [preact.reshape(rows, units, 2 * hid), back_grad.reshape(rows, units, 2 * hid)], axis=1
    )
    parts = lax.all_to_all(parts, "row", 0, 0)
    sums = jnp.sum(parts.astype(jnp.float32), axis=0)
    hidden, grad_pre = activate(sums[0], sums[1])
    pair = jnp.stack([hidden, grad_pre])
    spread = lax.all_to_all(jnp.broadcast_to(pair[None], (rows,) + pair.shape), "row", 0, 0)
    hidden = spread[:, 0].reshape(rows * units, 2 * hid)
    grad_pre = spread[:, 1].reshape(rows * units, 2 * hid)

    out_part = jnp.dot(hidden, w_down_all, preferred_element_type=jnp.float32)
    back_part = lax.dot_general(
        grad_pre, w_up_all, contract_last, preferred_element_type=jnp.float32
    )
    part = jnp.concatenate([out_part, back_part], axis=1)
    held = first.shape[0]
    blocks = [part[i * held : (i + 1) * held] for i in range(4)]

    def add(value, sent, perm):
        return value + swap(sent.astype(jnp.bfloat16), perm).astype(jnp.float32)

    acc = add(blocks[2], blocks[3], odd)
    acc = add(blocks[1], acc, even)
    acc = add(blocks[0], acc, odd)
    acc = add(acc[: held // 2], acc[held // 2 :], even)
    acc = add(acc[:share], acc[share:], swap_half)
    output = acc[:, :feats].astype(jnp.bfloat16)
    grad_tokens = acc[:, feats:].astype(jnp.bfloat16)

    both_other = swap(both, swap_core)
    acts_other = swap(jnp.stack([hidden[:, hid:], grad_pre[:, hid:]]), swap_core)
    both_all = jnp.concatenate([both, both_other], axis=0)
    hidden_all = jnp.concatenate([hidden[:, :hid], acts_other[0]], axis=0)
    grad_pre_all = jnp.concatenate([grad_pre[:, :hid], acts_other[1]], axis=0)
    grad_up = (
        lax.dot_general(
            both_all[:, :feats], grad_pre_all, contract_first, preferred_element_type=jnp.float32
        )
        * grad_scale
    ).astype(jnp.bfloat16)
    grad_down = (
        lax.dot_general(
            hidden_all, both_all[:, feats:], contract_first, preferred_element_type=jnp.float32
        )
        * grad_scale
    ).astype(jnp.bfloat16)
    return (output, grad_tokens, grad_up, grad_down)


def solution(mesh):
    placed = (P("col", "row"), P("row", "col"), P("col", "row"), P("col", "row"))
    rows, cols = mesh.shape["row"], mesh.shape["col"]
    swaps = perms(cols)

    def block(*args):
        return local(*swaps, rows, *args)

    return jax.shard_map(
        block,
        mesh=mesh,
        in_specs=placed,
        out_specs=(P("col", "row"), P("col", "row"), P("row", "col"), P("col", "row")),
        check_vma=False,
    )
```

```python
import math

import jax
import jax.numpy as jnp
from jax import lax
from jax.sharding import PartitionSpec as P

gelu_coef = 0.7978845608028654


def activate(preact, back_grad):
    tanh_val = jnp.tanh(gelu_coef * (preact + 0.044715 * preact * preact * preact))
    activated = 0.5 * preact * (1.0 + tanh_val)
    derivative = 0.5 * (1.0 + tanh_val) + 0.5 * preact * (1.0 - tanh_val * tanh_val) * gelu_coef * (
        1.0 + 3.0 * 0.044715 * preact * preact
    )
    return (activated.astype(jnp.bfloat16), (back_grad * derivative).astype(jnp.bfloat16))


def perms(cols):
    ring = cols // 4

    def index(x_hi, z, core):
        return (x_hi * ring + z % ring) * 2 + core

    places = [(h, z, c) for h in range(2) for z in range(ring) for c in range(2)]
    swap_core = [(index(h, z, c), index(h, z, 1 - c)) for h, z, c in places]
    swap_half = [(index(h, z, c), index(1 - h, z, c)) for h, z, c in places]

    def pairing(phase, across):
        def partner(z, c):
            return z + 1 if (z + c + phase) % 2 == 0 else z - 1

        return [(index(h, z, c), index(h ^ across, partner(z, c), c)) for h, z, c in places]

    pairs = [(pairing(phase, 0), pairing(phase, 1)) for phase in (0, 1)]
    return swap_core, swap_half, *pairs


def local(swap_core, swap_half, even, odd, rows, tokens, w_up, w_down, grad_out):
    contract_last = (((1,), (1,)), ((), ()))
    contract_first = (((0,), (0,)), ((), ()))

    def swap(value, perm):
        return lax.ppermute(value, "col", perm)

    share = tokens.shape[0]
    feats = tokens.shape[1]
    total_rows = share * len(swap_core)
    hid = w_up.shape[1]
    grad_scale = 1.0 / math.sqrt(total_rows)

    mine = jnp.concatenate([tokens, grad_out], axis=1)
    along = [mine, swap(mine, even[0])]
    across = [swap(mine, swap_half), swap(mine, even[1])]
    sent = jnp.concatenate(along, axis=0)
    got = swap(sent, odd[0])
    far = swap(sent, odd[1])
    got, *across = lax.optimization_barrier((got, *across))
    last = swap(got, even[0])
    far2 = swap(got, even[1])
    last, far = lax.optimization_barrier((last, far))
    along += [got, last, swap(last, odd[0])]
    across += [far, far2, swap(last, odd[1])]
    w_up_all = jnp.concatenate([w_up, swap(w_up, swap_core)], axis=1)
    w_down_all = jnp.concatenate([w_down, swap(w_down, swap_core)], axis=0)
    both = jnp.concatenate(along + across, axis=0)
    x_own, dy_own = both[:, :feats], both[:, feats:]
    units = both.shape[0] // rows

    preact = jnp.dot(x_own, w_up_all, preferred_element_type=jnp.float32).astype(jnp.bfloat16)
    back_grad = lax.dot_general(
        dy_own, w_down_all, contract_last, preferred_element_type=jnp.float32
    ).astype(jnp.bfloat16)
    parts = jnp.stack(
        [preact.reshape(rows, units, 2 * hid), back_grad.reshape(rows, units, 2 * hid)], axis=1
    )
    parts = lax.all_to_all(parts, "row", 0, 0)
    sums = jnp.sum(parts.astype(jnp.float32), axis=0)
    hidden, grad_pre = activate(sums[0], sums[1])
    pair = jnp.stack([hidden, grad_pre])
    spread = lax.all_to_all(jnp.broadcast_to(pair[None], (rows,) + pair.shape), "row", 0, 0)
    hidden = spread[:, 0].reshape(rows * units, 2 * hid)
    grad_pre = spread[:, 1].reshape(rows * units, 2 * hid)

    both, hidden, grad_pre = lax.optimization_barrier((both, hidden, grad_pre))
    acts_other = swap(jnp.stack([hidden[:, hid:], grad_pre[:, hid:]]), swap_core)
    both_other = swap(both, swap_core)
    grad_up = jnp.zeros((), jnp.float32)
    grad_down = jnp.zeros((), jnp.float32)
    for tok, h, g in (
        (both, hidden[:, :hid], grad_pre[:, :hid]),
        (both_other, acts_other[0], acts_other[1]),
    ):
        grad_up += lax.dot_general(
            tok[:, :feats], g, contract_first, preferred_element_type=jnp.float32
        )
        grad_down += lax.dot_general(
            h, tok[:, feats:], contract_first, preferred_element_type=jnp.float32
        )
    grad_up = (grad_up * grad_scale).astype(jnp.bfloat16)
    grad_down = (grad_down * grad_scale).astype(jnp.bfloat16)

    out_part = jnp.dot(hidden, w_down_all, preferred_element_type=jnp.float32)
    back_part = lax.dot_general(
        grad_pre, w_up_all, contract_last, preferred_element_type=jnp.float32
    )
    part = jnp.concatenate([out_part, back_part], axis=1)
    half = total_rows // 4
    held = 2 * share
    along = [part[i * held : (i + 1) * held] for i in range(4)]
    across = [part[half + i * held : half + (i + 1) * held] for i in range(4)]

    def add(value, sent, perm):
        return value + swap(sent.astype(jnp.bfloat16), perm).astype(jnp.float32)

    acc = add(add(along[2], across[3], odd[1]), along[3], odd[0])
    acc, grad_down = lax.optimization_barrier((add(add(along[1], across[2], even[1]), acc, even[0]), grad_down))
    acc, grad_up = lax.optimization_barrier((add(add(along[0], across[1], odd[1]), acc, odd[0]), grad_up))
    own = add(acc[:share], across[0][:share], swap_half)
    own = add(own, across[0][share:], even[1])
    acc = add(own, acc[share:], even[0])
    output = acc[:, :feats].astype(jnp.bfloat16)
    grad_tokens = acc[:, feats:].astype(jnp.bfloat16)
    return (output, grad_tokens, grad_up, grad_down)


def solution(mesh):
    placed = (P("col", "row"), P("row", "col"), P("col", "row"), P("col", "row"))
    rows, cols = mesh.shape["row"], mesh.shape["col"]
    swaps = perms(cols)

    def block(*args):
        return local(*swaps, rows, *args)

    return jax.shard_map(
        block,
        mesh=mesh,
        in_specs=placed,
        out_specs=(P("col", "row"), P("col", "row"), P("row", "col"), P("col", "row")),
        check_vma=False,
    )
```

```python
import math

import jax
import jax.numpy as jnp
from jax import lax
from jax.sharding import PartitionSpec as P

gelu_coef = 0.7978845608028654


def activate(preact, back_grad):
    tanh_val = jnp.tanh(gelu_coef * (preact + 0.044715 * preact * preact * preact))
    activated = 0.5 * preact * (1.0 + tanh_val)
    derivative = 0.5 * (1.0 + tanh_val) + 0.5 * preact * (1.0 - tanh_val * tanh_val) * gelu_coef * (
        1.0 + 3.0 * 0.044715 * preact * preact
    )
    return (activated.astype(jnp.bfloat16), (back_grad * derivative).astype(jnp.bfloat16))


def perms(cols):
    ring = cols // 4

    def index(x_hi, z, core):
        return (x_hi * ring + z % ring) * 2 + core

    places = [(h, z, c) for h in range(2) for z in range(ring) for c in range(2)]
    swap_core = [(index(h, z, c), index(h, z, 1 - c)) for h, z, c in places]
    swap_half = [(index(h, z, c), index(1 - h, z, c)) for h, z, c in places]

    def pairing(phase, across):
        def partner(z, c):
            return z + 1 if (z + c + phase) % 2 == 0 else z - 1

        return [(index(h, z, c), index(h ^ across, partner(z, c), c)) for h, z, c in places]

    pairs = [(pairing(phase, 0), pairing(phase, 1)) for phase in (0, 1)]
    return swap_core, swap_half, *pairs


def local(swap_core, swap_half, even, odd, rows, tokens, w_up, w_down, grad_out):
    contract_last = (((1,), (1,)), ((), ()))
    contract_first = (((0,), (0,)), ((), ()))

    def swap(value, perm):
        return lax.ppermute(value, "col", perm)

    share = tokens.shape[0]
    feats = tokens.shape[1]
    total_rows = share * len(swap_core)
    hid = w_up.shape[1]
    grad_scale = 1.0 / math.sqrt(total_rows)

    def after(value, *others):
        return lax.optimization_barrier((value, *others))[0]

    mine = jnp.concatenate([tokens, grad_out], axis=1)
    near1 = swap(mine, even[0])
    far0 = swap(mine, swap_half)
    far1 = swap(mine, even[1])
    near01 = jnp.concatenate([mine, near1], axis=0)
    near2 = swap(near01, odd[0])
    far2 = swap(near01, odd[1])
    near2, far0, far1 = lax.optimization_barrier((near2, far0, far1))
    near3 = swap(near2, even[0])
    far3 = swap(near2, even[1])
    near3, far2 = lax.optimization_barrier((near3, far2))
    near4 = swap(near3, odd[0])
    far4 = swap(near3, odd[1])
    w_up, w_down = lax.optimization_barrier((w_up, w_down, near2))[:2]
    w_up_all = jnp.concatenate([w_up, swap(w_up, swap_core)], axis=1)
    w_down_all = jnp.concatenate([w_down, swap(w_down, swap_core)], axis=0)
    both = jnp.concatenate([near01, far0, far1, near2, far2, near3, far3, near4, far4], axis=0)
    x_own, dy_own = both[:, :feats], both[:, feats:]
    units = both.shape[0] // rows

    preact = jnp.dot(x_own, w_up_all, preferred_element_type=jnp.float32).astype(jnp.bfloat16)
    back_grad = lax.dot_general(
        dy_own, w_down_all, contract_last, preferred_element_type=jnp.float32
    ).astype(jnp.bfloat16)
    parts = jnp.stack(
        [preact.reshape(rows, units, 2 * hid), back_grad.reshape(rows, units, 2 * hid)], axis=1
    )
    parts = lax.all_to_all(parts, "row", 0, 0)
    sums = jnp.sum(parts.astype(jnp.float32), axis=0)
    hidden, grad_pre = activate(sums[0], sums[1])
    pair = jnp.stack([hidden, grad_pre])
    spread = lax.all_to_all(jnp.broadcast_to(pair[None], (rows,) + pair.shape), "row", 0, 0)
    hidden = spread[:, 0].reshape(rows * units, 2 * hid)
    grad_pre = spread[:, 1].reshape(rows * units, 2 * hid)

    both, hidden, grad_pre = lax.optimization_barrier((both, hidden, grad_pre))

    out_part = jnp.dot(hidden, w_down_all, preferred_element_type=jnp.float32)
    back_part = lax.dot_general(
        grad_pre, w_up_all, contract_last, preferred_element_type=jnp.float32
    )
    part = jnp.concatenate([out_part, back_part], axis=1)
    held = 2 * share

    def rows_of(i, j):
        return jnp.concatenate([part[k * share : (k + 1) * share] for k in (i, j)], axis=0)


    def moved(sent, perm, *others):
        return swap(after(sent.astype(jnp.bfloat16), *others), perm)

    near01, far01 = rows_of(0, 4), rows_of(2, 6)
    near2, far2 = rows_of(1, 8), rows_of(3, 10)
    near3, far3 = rows_of(5, 12), rows_of(7, 14)
    near4, far4 = rows_of(9, 13), rows_of(11, 15)
    far4 = moved(far4, even[1])
    near3 = near3 + far4 + moved(near4, even[0])

    acts_sent = jnp.stack([hidden[:, hid:], grad_pre[:, hid:]])
    acts_other = swap(after(acts_sent, near3), swap_core)
    both_other = swap(after(both, near3), swap_core)
    grad_up = grad_down = 0.0
    for tok, h, g in (
        (both, hidden[:, :hid], grad_pre[:, :hid]),
        (both_other, acts_other[0], acts_other[1]),
    ):
        grad_up += lax.dot_general(
            tok[:, :feats], g, contract_first, preferred_element_type=jnp.float32
        )
        grad_down += lax.dot_general(
            h, tok[:, feats:], contract_first, preferred_element_type=jnp.float32
        )
    grad_up = (grad_up * grad_scale).astype(jnp.bfloat16)
    grad_down = (grad_down * grad_scale).astype(jnp.bfloat16)

    far3 = moved(far3, odd[1], far4)
    near2 = near2 + far3 + moved(near3, odd[0])
    far2 = moved(far2, even[1], far3)
    far0 = moved(far01[:share], swap_half, far4)
    far1 = moved(far01[share:], odd[1], far3)
    near01 = near01 + far2 + moved(near2, even[0])
    acc = near01[:share] + far0 + far1
    near1 = moved(near01[share:], odd[0])
    near1, grad_down = lax.optimization_barrier((near1, grad_down))
    near1, grad_up = lax.optimization_barrier((near1, grad_up))
    acc = acc + near1
    output = acc[:, :feats].astype(jnp.bfloat16)
    grad_tokens = acc[:, feats:].astype(jnp.bfloat16)
    return (output, grad_tokens, grad_up, grad_down)


def solution(mesh):
    placed = (P("col", "row"), P("row", "col"), P("col", "row"), P("col", "row"))
    rows, cols = mesh.shape["row"], mesh.shape["col"]
    swaps = perms(cols)

    def block(*args):
        return local(*swaps, rows, *args)

    return jax.shard_map(
        block,
        mesh=mesh,
        in_specs=placed,
        out_specs=(P("col", "row"), P("col", "row"), P("row", "col"), P("col", "row")),
        check_vma=False,
    )
```

```python
import math

import jax
import jax.numpy as jnp
from jax import lax
from jax.sharding import PartitionSpec as P

gelu_coef = 0.7978845608028654


def activate(preact, back_grad):
    tanh_val = jnp.tanh(gelu_coef * (preact + 0.044715 * preact * preact * preact))
    activated = 0.5 * preact * (1.0 + tanh_val)
    derivative = 0.5 * (1.0 + tanh_val) + 0.5 * preact * (1.0 - tanh_val * tanh_val) * gelu_coef * (
        1.0 + 3.0 * 0.044715 * preact * preact
    )
    return (activated.astype(jnp.bfloat16), (back_grad * derivative).astype(jnp.bfloat16))


def perms(cols):
    ring = cols // 4

    def index(x_hi, z, core):
        return (x_hi * ring + z % ring) * 2 + core

    places = [(h, z, c) for h in range(2) for z in range(ring) for c in range(2)]
    swap_core = [(index(h, z, c), index(h, z, 1 - c)) for h, z, c in places]
    swap_half = [(index(h, z, c), index(1 - h, z, c)) for h, z, c in places]

    def pairing(phase, across):
        def partner(z, c):
            return z + 1 if (z + c + phase) % 2 == 0 else z - 1

        return [(index(h, z, c), index(h ^ across, partner(z, c), c)) for h, z, c in places]

    pairs = [(pairing(phase, 0), pairing(phase, 1)) for phase in (0, 1)]
    return swap_core, swap_half, *pairs


def local(swap_core, swap_half, even, odd, rows, tokens, w_up, w_down, grad_out):
    contract_last = (((1,), (1,)), ((), ()))
    contract_first = (((0,), (0,)), ((), ()))

    def swap(value, perm):
        return lax.ppermute(value, "col", perm)

    share = tokens.shape[0]
    feats = tokens.shape[1]
    total_rows = share * len(swap_core)
    hid = w_up.shape[1]
    grad_scale = 1.0 / math.sqrt(total_rows)

    def after(value, *others):
        return lax.optimization_barrier((value, *others))[0]

    mine = jnp.concatenate([tokens, grad_out], axis=1)
    near1 = swap(mine, even[0])
    far0 = swap(mine, swap_half)
    far1 = swap(mine, even[1])
    near01 = jnp.concatenate([mine, near1], axis=0)
    near2 = swap(near01, odd[0])
    far2 = swap(near01, odd[1])
    near2, far0, far1 = lax.optimization_barrier((near2, far0, far1))
    near3 = swap(near2, even[0])
    far3 = swap(near2, even[1])
    near3, far2 = lax.optimization_barrier((near3, far2))
    near4 = swap(near3, odd[0])
    far4 = swap(near3, odd[1])
    w_up, w_down = lax.optimization_barrier((w_up, w_down, near2))[:2]
    w_up_all = jnp.concatenate([w_up, swap(w_up, swap_core)], axis=1)
    w_down_all = jnp.concatenate([w_down, swap(w_down, swap_core)], axis=0)
    both = jnp.concatenate([near01, far0, far1, near2, far2, near3, far3, near4, far4], axis=0)
    x_own, dy_own = both[:, :feats], both[:, feats:]
    units = both.shape[0] // rows

    preact = jnp.dot(x_own, w_up_all, preferred_element_type=jnp.float32).astype(jnp.bfloat16)
    back_grad = lax.dot_general(
        dy_own, w_down_all, contract_last, preferred_element_type=jnp.float32
    ).astype(jnp.bfloat16)
    parts = jnp.stack(
        [preact.reshape(rows, units, 2 * hid), back_grad.reshape(rows, units, 2 * hid)], axis=1
    )
    parts = lax.all_to_all(parts, "row", 0, 0)
    sums = jnp.sum(parts.astype(jnp.float32), axis=0)
    hidden, grad_pre = activate(sums[0], sums[1])
    pair = jnp.stack([hidden, grad_pre])
    spread = lax.all_to_all(jnp.broadcast_to(pair[None], (rows,) + pair.shape), "row", 0, 0)
    hidden = spread[:, 0].reshape(rows * units, 2 * hid)
    grad_pre = spread[:, 1].reshape(rows * units, 2 * hid)

    both, hidden, grad_pre = lax.optimization_barrier((both, hidden, grad_pre))

    out_part = jnp.dot(hidden, w_down_all, preferred_element_type=jnp.float32)
    back_part = lax.dot_general(
        grad_pre, w_up_all, contract_last, preferred_element_type=jnp.float32
    )
    part = jnp.concatenate([out_part, back_part], axis=1)
    held = 2 * share

    def rows_of(i, j):
        return jnp.concatenate([part[k * share : (k + 1) * share] for k in (i, j)], axis=0)


    def moved(sent, perm, *others):
        return swap(after(sent.astype(jnp.bfloat16), *others), perm)

    near01, far01 = rows_of(0, 4), rows_of(2, 6)
    near2, far2 = rows_of(1, 8), rows_of(3, 10)
    near3, far3 = rows_of(5, 12), rows_of(7, 14)
    near4, far4 = rows_of(9, 13), rows_of(11, 15)
    near3 = near3 + moved(far4, even[1]) + moved(near4, even[0])

    acts_sent = jnp.stack([hidden[:, hid:], grad_pre[:, hid:]])
    acts_other = swap(after(acts_sent, near3), swap_core)
    both_other = swap(after(both, near3), swap_core)
    grad_up = grad_down = 0.0
    for tok, h, g in (
        (both, hidden[:, :hid], grad_pre[:, :hid]),
        (both_other, acts_other[0], acts_other[1]),
    ):
        grad_up += lax.dot_general(
            tok[:, :feats], g, contract_first, preferred_element_type=jnp.float32
        )
        grad_down += lax.dot_general(
            h, tok[:, feats:], contract_first, preferred_element_type=jnp.float32
        )
    grad_up = (grad_up * grad_scale).astype(jnp.bfloat16)
    grad_down = (grad_down * grad_scale).astype(jnp.bfloat16)

    far2 = far2 + moved(far3, odd[0])
    near2 = near2 + moved(near3, odd[0])
    far01 = far01 + moved(far2, even[0])
    near01 = near01 + moved(near2, even[0])
    far0 = far01[:share] + moved(far01[share:], odd[0])
    acc = near01[:share] + moved(far0, swap_half)
    near1 = moved(near01[share:], odd[0])
    near1, grad_down = lax.optimization_barrier((near1, grad_down))
    near1, grad_up = lax.optimization_barrier((near1, grad_up))
    acc = acc + near1
    output = acc[:, :feats].astype(jnp.bfloat16)
    grad_tokens = acc[:, feats:].astype(jnp.bfloat16)
    return (output, grad_tokens, grad_up, grad_down)


def solution(mesh):
    placed = (P("col", "row"), P("row", "col"), P("col", "row"), P("col", "row"))
    rows, cols = mesh.shape["row"], mesh.shape["col"]
    swaps = perms(cols)

    def block(*args):
        return local(*swaps, rows, *args)

    return jax.shard_map(
        block,
        mesh=mesh,
        in_specs=placed,
        out_specs=(P("col", "row"), P("col", "row"), P("row", "col"), P("col", "row")),
        check_vma=False,
    )
```

```python
import math

import jax
import jax.numpy as jnp
from jax import lax
from jax.sharding import PartitionSpec as P

gelu_coef = 0.7978845608028654


def activate(preact, back_grad):
    tanh_val = jnp.tanh(gelu_coef * (preact + 0.044715 * preact * preact * preact))
    activated = 0.5 * preact * (1.0 + tanh_val)
    derivative = 0.5 * (1.0 + tanh_val) + 0.5 * preact * (1.0 - tanh_val * tanh_val) * gelu_coef * (
        1.0 + 3.0 * 0.044715 * preact * preact
    )
    return (activated.astype(jnp.bfloat16), (back_grad * derivative).astype(jnp.bfloat16))


def perms(cols):
    ring = cols // 4

    def index(x_hi, z, core):
        return (x_hi * ring + z % ring) * 2 + core

    places = [(h, z, c) for h in range(2) for z in range(ring) for c in range(2)]
    swap_core = [(index(h, z, c), index(h, z, 1 - c)) for h, z, c in places]
    swap_half = [(index(h, z, c), index(1 - h, z, c)) for h, z, c in places]

    def pairing(phase, across):
        def partner(z, c):
            return z + 1 if (z + c + phase) % 2 == 0 else z - 1

        return [(index(h, z, c), index(h ^ across, partner(z, c), c)) for h, z, c in places]

    pairs = [(pairing(phase, 0), pairing(phase, 1)) for phase in (0, 1)]
    return swap_core, swap_half, *pairs


def local(swap_core, swap_half, even, odd, rows, tokens, w_up, w_down, grad_out):
    contract_last = (((1,), (1,)), ((), ()))
    contract_first = (((0,), (0,)), ((), ()))

    def swap(value, perm):
        return lax.ppermute(value, "col", perm)

    share = tokens.shape[0]
    feats = tokens.shape[1]
    total_rows = share * len(swap_core)
    hid = w_up.shape[1]
    grad_scale = 1.0 / math.sqrt(total_rows)

    def after(value, *others):
        return lax.optimization_barrier((value, *others))[0]

    mine = jnp.concatenate([tokens, grad_out], axis=1)
    near1 = swap(mine, even[0])
    far0 = swap(mine, swap_half)
    near01 = jnp.concatenate([mine, near1], axis=0)
    near2 = swap(near01, odd[0])
    far1 = swap(far0, even[0])
    far01 = jnp.concatenate([far0, far1], axis=0)
    near3 = swap(near2, even[0])
    far2 = swap(far01, odd[0])
    near4 = swap(near3, odd[0])
    far4 = swap(near3, odd[1])
    far3 = swap(far2, even[0])
    w_up, w_down = lax.optimization_barrier((w_up, w_down, near3))[:2]
    w_up_all = jnp.concatenate([w_up, swap(w_up, swap_core)], axis=1)
    w_down_all = jnp.concatenate([w_down, swap(w_down, swap_core)], axis=0)
    both = jnp.concatenate([near01, far01, near2, far2, near3, far3, near4, far4], axis=0)
    x_own, dy_own = both[:, :feats], both[:, feats:]
    units = both.shape[0] // rows

    preact = jnp.dot(x_own, w_up_all, preferred_element_type=jnp.float32).astype(jnp.bfloat16)
    back_grad = lax.dot_general(
        dy_own, w_down_all, contract_last, preferred_element_type=jnp.float32
    ).astype(jnp.bfloat16)
    parts = jnp.stack(
        [preact.reshape(rows, units, 2 * hid), back_grad.reshape(rows, units, 2 * hid)], axis=1
    )
    parts = lax.all_to_all(parts, "row", 0, 0)
    sums = jnp.sum(parts.astype(jnp.float32), axis=0)
    hidden, grad_pre = activate(sums[0], sums[1])
    pair = jnp.stack([hidden, grad_pre])
    spread = lax.all_to_all(jnp.broadcast_to(pair[None], (rows,) + pair.shape), "row", 0, 0)
    hidden = spread[:, 0].reshape(rows * units, 2 * hid)
    grad_pre = spread[:, 1].reshape(rows * units, 2 * hid)

    both, hidden, grad_pre = lax.optimization_barrier((both, hidden, grad_pre))

    out_part = jnp.dot(hidden, w_down_all, preferred_element_type=jnp.float32)
    back_part = lax.dot_general(
        grad_pre, w_up_all, contract_last, preferred_element_type=jnp.float32
    )
    part = jnp.concatenate([out_part, back_part], axis=1)
    held = 2 * share

    def rows_of(i, j):
        return jnp.concatenate([part[k * share : (k + 1) * share] for k in (i, j)], axis=0)


    def moved(sent, perm, *others):
        return swap(after(sent.astype(jnp.bfloat16), *others), perm)

    near01, far01 = rows_of(0, 4), rows_of(2, 6)
    near2, far2 = rows_of(1, 8), rows_of(3, 10)
    near3, far3 = rows_of(5, 12), rows_of(7, 14)
    near4, far4 = rows_of(9, 13), rows_of(11, 15)
    near3 = near3 + moved(far4, even[1]) + moved(near4, even[0])

    acts_sent = jnp.stack([hidden[:, hid:], grad_pre[:, hid:]])
    acts_other = swap(after(acts_sent, near3), swap_core)
    both_other = swap(after(both, near3), swap_core)
    grad_up = grad_down = 0.0
    for tok, h, g in (
        (both, hidden[:, :hid], grad_pre[:, :hid]),
        (both_other, acts_other[0], acts_other[1]),
    ):
        grad_up += lax.dot_general(
            tok[:, :feats], g, contract_first, preferred_element_type=jnp.float32
        )
        grad_down += lax.dot_general(
            h, tok[:, feats:], contract_first, preferred_element_type=jnp.float32
        )
    grad_up = (grad_up * grad_scale).astype(jnp.bfloat16)
    grad_down = (grad_down * grad_scale).astype(jnp.bfloat16)

    far2 = far2 + moved(far3, odd[0])
    near2 = near2 + moved(near3, odd[0])
    far01 = far01 + moved(far2, even[0])
    near01 = near01 + moved(near2, even[0])
    far0 = far01[:share] + moved(far01[share:], odd[0])
    acc = near01[:share] + moved(far0, swap_half)
    near1 = moved(near01[share:], odd[0])
    near1, grad_down = lax.optimization_barrier((near1, grad_down))
    near1, grad_up = lax.optimization_barrier((near1, grad_up))
    acc = acc + near1
    output = acc[:, :feats].astype(jnp.bfloat16)
    grad_tokens = acc[:, feats:].astype(jnp.bfloat16)
    return (output, grad_tokens, grad_up, grad_down)


def solution(mesh):
    placed = (P("col", "row"), P("row", "col"), P("col", "row"), P("col", "row"))
    rows, cols = mesh.shape["row"], mesh.shape["col"]
    swaps = perms(cols)

    def block(*args):
        return local(*swaps, rows, *args)

    return jax.shard_map(
        block,
        mesh=mesh,
        in_specs=placed,
        out_specs=(P("col", "row"), P("col", "row"), P("row", "col"), P("col", "row")),
        check_vma=False,
    )
```
